1024 devices in a mesh: dp: 16 (over z_lo, core), mp: 64 (over y, x, z_hi).
Axes of the slice: x: 4, y: 4, z: 32 (z_hi: 4, z_lo: 8; z = z_hi * 8 + z_lo), core: 2. Of those that a mesh axis runs over, the one named last changes fastest.
Arguments:
- hidden_rows: bfloat16 [3008, 8192], P('dp'), may hold values from -6 to 6
- query_weight: bfloat16 [8192, 8192], P('dp', 'mp'), may hold values from -0.0625 to 0.0625
- output_weight: bfloat16 [8192, 8192], P('mp'), may hold values from -0.375 to 0.375
- new_kv: bfloat16 [2, 3008, 1024], P(None, 'dp'), may hold values from -6 to 6
- prefix_kv: bfloat16 [2, 752, 8, 16, 128], P(None, 'dp'), may hold values from -300 to 300
- adapter_bank: bfloat16 [752, 2, 8, 8192], P('dp', None, None, 'mp'), may hold values from -0.69921875 to 0.69921875
- send_plan: int32 [16, 16, 5], P('dp'), may hold values from 0 to 46, as said below
- user_slot: int32 [752], P('dp'), may hold values from 0 to 79, as said below
Outputs:
- mixed: bfloat16 [3008, 8192], P('dp', 'mp')
The draws below stay inside these ranges and needn't reach their ends.
Inputs may be any that keep to these rules, and one draw needn't show every extreme that they name: send_plan[s, g, c] is an index into owner group s's 47 adapters. Slots c below the number of g's users served by s name distinct adapters; the other slots hold valid indices that no user reads. Each of an owner's adapters is read by exactly one user. user_slot[u] = s * 5 + c means the adapter of user u (of row group g = u // 47) is send_plan[s, g, c] of owner group s. Users of one group have distinct slots and use their owner's slots from c = 0 upward. The number of group g's users served by owner s depends only on (s - g) mod 16; it is exactly 5 at distance 0 and at one or more other distances, and at most 5 everywhere.
All inputs are finite; a program needn't handle non-finite values.
Results may differ from the reference program's by a relative error of at most 0.009.
Values may be sent and summed in bfloat16 or wider, within the bound.
A program may use at most 64 MiB of HBM per device.

```python
import math
import jax
import jax.numpy as jnp
from jax import lax

D = 8192
H = 64
KV_HEADS = 8
HD = 128
RANK = 8
SAMPLES = 4
USERS_DEV = 47
PREFIX = 16
GROUP = 8
USERS = 752
ROWS = 3008
CAP = 5
N_DP = 16


def plan_tables(key):
    group_total = N_DP
    user_total = USERS_DEV
    spare = user_total - CAP
    others = group_total - 1
    floor_load = min(1, spare // others)
    rest = spare - floor_load * others
    priority = jax.random.permutation(jax.random.fold_in(key, 11), others).astype(jnp.int32)
    priority = priority.at[group_total // 2 - 1].set(-1)
    priority = priority.at[others - 1].set(-2)
    ordering = jnp.argsort(priority, stable=True).astype(jnp.int32)
    rank_ids = jnp.arange(others, dtype=jnp.int32)
    by_rank = floor_load + jnp.clip(rest - rank_ids * (CAP - floor_load), 0, CAP - floor_load)
    extra_load = jnp.zeros((others,), jnp.int32).at[ordering].set(by_rank.astype(jnp.int32))
    spread = jnp.concatenate([jnp.full((1,), CAP, jnp.int32), extra_load.astype(jnp.int32)])
    source = jnp.arange(group_total, dtype=jnp.int32)[:, None]
    target = jnp.arange(group_total, dtype=jnp.int32)[None, :]
    counts = spread[(source - target) % group_total]
    ends = jnp.cumsum(counts, axis=0)
    starts = ends - counts
    position = jnp.arange(user_total, dtype=jnp.int32)
    owner = jnp.sum((position[None, :, None] >= ends[:, None, :]).astype(jnp.int32), axis=0)
    owner_start = starts[owner, jnp.arange(group_total, dtype=jnp.int32)[None, :]]
    slot_value = owner * CAP + position[:, None] - owner_start
    user_keys = jax.random.split(jax.random.fold_in(key, 12), group_total)
    user_order = jax.vmap(lambda sub_key: jax.random.permutation(sub_key, user_total))(user_keys).astype(jnp.int32)
    row_ids = jnp.arange(group_total, dtype=jnp.int32)[:, None]
    user_slot = jnp.zeros((group_total, user_total), jnp.int32).at[row_ids, user_order].set(slot_value.T)
    owned_keys = jax.random.split(jax.random.fold_in(key, 13), group_total)
    owned = jax.vmap(lambda sub_key: jax.random.permutation(sub_key, user_total))(owned_keys).astype(jnp.int32)
    offsets = jnp.cumsum(counts, axis=1) - counts
    slot_ids = jnp.arange(CAP, dtype=jnp.int32)[None, None, :]
    within = jnp.minimum(slot_ids, jnp.maximum(counts[:, :, None] - 1, 0))
    pick_ids = jnp.minimum(offsets[:, :, None] + within, user_total - 1)
    send_plan = owned[jnp.arange(group_total, dtype=jnp.int32)[:, None, None], pick_ids]
    return (send_plan.astype(jnp.int32), user_slot.reshape(group_total * user_total).astype(jnp.int32))


def draw_send_plan(key, part):
    tables = plan_tables(key)
    return tables[0]


def draw_user_slot(key, part):
    tables = plan_tables(key)
    return tables[1]


def draw_prefix_kv(key, part):
    key = jax.random.fold_in(key, 5)
    user_total = USERS_DEV * N_DP
    shape = (2, user_total, KV_HEADS, PREFIX, HD)
    cache = jnp.clip(jax.random.normal(key, shape, jnp.float32), -6.0, 6.0)
    return cache.astype(jnp.bfloat16)


def block_scale(key, shape, cuts, least, top_value):
    level, own = 1.0, jax.random.fold_in(key, 6)
    for dim, shards_of in cuts:
        heights = jnp.exp(jax.random.uniform(jax.random.fold_in(own, dim), (shards_of,), jnp.float32, least / len(cuts), top_value / len(cuts)))
        level = level * jnp.repeat(heights, shape[dim] // shards_of).reshape([-1 if axis == dim else 1 for axis in range(len(shape))])
    return level


def noise(stream_key, extent, scale, reach, shards=(), held_as=jnp.bfloat16):
    values = scale * jax.random.normal(stream_key, extent, jnp.float32)
    if shards:
        values = values * block_scale(stream_key, extent, shards, -0.22, 0.18)
    return jnp.clip(values, -reach, reach).astype(held_as)


def setup_inputs(seed: int = 0) -> dict:
    key_list = jax.random.split(jax.random.key(seed), 9)
    hidden_rows = noise(key_list[0], (ROWS, D), 1.0, 6.0, ((0, 16),))
    query_weight = noise(key_list[1], (D, H * HD), D ** -0.5, 0.0625, ((0, 16), (1, 64)))
    output_weight = noise(key_list[2], (H * HD, D), (D // 32) ** -0.5, 0.375, ((0, 64),))
    new_kv = noise(key_list[3], (2, ROWS, KV_HEADS * HD), 1.0, 6.0, ((1, 16),))
    prefix_kv = draw_prefix_kv(jax.random.fold_in(key_list[8], 71), 0)
    adapter_bank = noise(key_list[5], (USERS, 2, RANK, D), 0.12, 0.69921875, ((0, 16), (3, 64)))
    send_plan = draw_send_plan(jax.random.fold_in(key_list[8], 71), 0)
    user_slot = draw_user_slot(jax.random.fold_in(key_list[8], 71), 0)
    return {"hidden_rows": hidden_rows, "query_weight": query_weight, "output_weight": output_weight, "new_kv": new_kv, "prefix_kv": prefix_kv, "adapter_bank": adapter_bank, "send_plan": send_plan, "user_slot": user_slot}


def adapter_index(send_plan, user_slot):
    user_ids = jnp.arange(user_slot.shape[0], dtype=jnp.int32)
    group_ids = user_ids // USERS_DEV
    source = user_slot // CAP
    place_ids = user_slot % CAP
    local_ids = send_plan[source, group_ids, place_ids]
    return (source * USERS_DEV + local_ids).astype(jnp.int32)

def attend_user(bundle):
    query_user, key_user, value_user, own_key, own_value = bundle
    score_scale = 1.0 / math.sqrt(HD)
    query_heads = query_user.reshape(SAMPLES, KV_HEADS, GROUP, HD).astype(jnp.float32)
    own_keys = own_key.reshape(SAMPLES, KV_HEADS, HD).astype(jnp.float32)
    own_values = own_value.reshape(SAMPLES, KV_HEADS, HD).astype(jnp.float32)
    cached = jnp.einsum('skgd,kpd->skgp', query_heads, key_user.astype(jnp.float32)) * score_scale
    own_score = lax.optimization_barrier(jnp.sum(query_heads * own_keys[:, :, None, :], axis=-1)) * score_scale
    row_top = jnp.maximum(lax.optimization_barrier(jnp.max(cached, axis=-1)), own_score)
    cached_exp = jnp.exp(cached - row_top[..., None])
    own_exp = jnp.exp(own_score - row_top)
    weight_total = lax.optimization_barrier(jnp.sum(cached_exp, axis=-1)) + own_exp
    cached_weight = (cached_exp / weight_total[..., None]).astype(jnp.bfloat16)
    own_weight = (own_exp / weight_total).astype(jnp.bfloat16)
    mixed_values = jnp.einsum('skgp,kpd->skgd', cached_weight.astype(jnp.float32), value_user.astype(jnp.float32))
    mixed_values = mixed_values + own_weight.astype(jnp.float32)[..., None] * own_values[:, :, None, :]
    return mixed_values.astype(jnp.bfloat16).reshape(SAMPLES, H * HD)

def reference(hidden_rows, query_weight, output_weight, new_kv, prefix_kv, adapter_bank, send_plan, user_slot):
    queries = jnp.dot(hidden_rows, query_weight, preferred_element_type=jnp.float32).astype(jnp.bfloat16)
    user_total = user_slot.shape[0]
    bundle = (queries.reshape(user_total, SAMPLES, H * HD), prefix_kv[0], prefix_kv[1], new_kv[0].reshape(user_total, SAMPLES, KV_HEADS * HD), new_kv[1].reshape(user_total, SAMPLES, KV_HEADS * HD))
    attended = lax.map(attend_user, bundle).reshape(user_total * SAMPLES, H * HD)
    adapters = adapter_bank[adapter_index(send_plan, user_slot)]
    grouped = attended.reshape(user_total, SAMPLES, H * HD).astype(jnp.float32)
    rank_vector = jnp.einsum('usk,urk->usr', grouped, adapters[:, 0].astype(jnp.float32)).astype(jnp.bfloat16)
    adapter_out = jnp.einsum('usr,urk->usk', rank_vector.astype(jnp.float32), adapters[:, 1].astype(jnp.float32))
    base_out = jnp.dot(attended, output_weight, preferred_element_type=jnp.float32)
    return (base_out + adapter_out.reshape(user_total * SAMPLES, D)).astype(jnp.bfloat16)
```

```python
import functools
import math

import jax
import jax.numpy as jnp
from jax import lax
from jax.experimental import pallas as pl
from jax.experimental.pallas import tpu as pltpu
from jax.sharding import PartitionSpec as P

SAMPLES = 4
GROUP = 8
CAP = 5
CORES = 2
Z_HI = 4
CHUNKS = 2
F32 = jnp.float32
BF16 = jnp.bfloat16


def each(first, last, step):
    def wrapped(i, carry):
        step(i)
        return carry

    lax.fori_loop(first, last, wrapped, 0)


def kernel(
    group,
    plan_ref, slot_ref, hid_hbm, qw_hbm, ow_hbm, new_hbm, prefix_hbm, bank_hbm,
    out_ref,
    hid, qbuf, acc, wbuf, fresh, cache, bank, give, take, qrows, att, part, zsend, zrecv,
    rank_xy, rank_z,
    local_sem, up_send, up_recv, down_send, down_recv, sib_send, sib_recv,
    w_send, w_recv, wsib_send, wsib_recv, give_send, take_recv, att_send, att_recv,
    z_send, z_recv, rxy_send, rxy_recv, rz_send, rz_recv,
):
    n_dp = qbuf.shape[0]
    n_xy = wbuf.shape[0]
    n_line = n_dp // CORES
    rows = hid.shape[0]
    shard = qbuf.shape[1]
    hd = qbuf.shape[2]
    users = cache.shape[1]
    prefix = cache.shape[2]
    pad_rows = att.shape[1]
    half = hd // CORES
    wide = wbuf.shape[2]
    bit = shard // CHUNKS

    me = lax.axis_index("dp")
    mp = lax.axis_index("mp")
    z, core = me // CORES, me % CORES
    spot, z_hi = mp // Z_HI, mp % Z_HI
    twin = z * CORES + (1 - core)
    kv = mp // group

    def dp_peer(d):
        return (me + d) % n_dp

    def xy_peer(d):
        return ((spot + d) % n_xy) * Z_HI + z_hi

    def z_peer(d):
        return spot * Z_HI + (z_hi + d) % Z_HI

    loads = [
        pltpu.make_async_copy(hid_hbm, hid, local_sem.at[0]),
        pltpu.make_async_copy(qw_hbm, qbuf.at[me], local_sem.at[1]),
        pltpu.make_async_copy(
            ow_hbm.at[:, pl.ds(pl.multiple_of(spot * wide, wide), wide)], wbuf.at[spot], local_sem.at[2]
        ),
        pltpu.make_async_copy(
            new_hbm.at[:, :, pl.ds(pl.multiple_of(kv * hd, hd), hd)], fresh, local_sem.at[3]
        ),
        pltpu.make_async_copy(prefix_hbm.at[:, :, kv], cache.at[:, pl.ds(0, prefix_hbm.shape[1])], local_sem.at[4]),
        pltpu.make_async_copy(bank_hbm, bank, local_sem.at[5]),
    ]
    for load in loads:
        load.start()

    barrier = pltpu.get_barrier_semaphore()

    def greet(peer):
        pl.semaphore_signal(barrier, inc=1, device_id=peer, device_id_type=pl.DeviceIdType.MESH)

    each(1, n_dp, lambda d: greet({"dp": dp_peer(d)}))
    each(1, n_xy, lambda d: greet({"mp": xy_peer(d)}))
    each(1, Z_HI, lambda d: greet({"mp": z_peer(d)}))
    pl.semaphore_wait(barrier, n_dp + n_xy + Z_HI - 3)

    def remote(src, dst, send_sem, recv_sem, peer):
        return pltpu.make_async_remote_copy(
            src_ref=src, dst_ref=dst, send_sem=send_sem, recv_sem=recv_sem,
            device_id=peer, device_id_type=pl.DeviceIdType.MESH,
        )

    def piece(origin, b):
        return qbuf.at[origin * CORES + core, pl.ds(b * bit, bit)]

    def up(i, b, src=None):
        dst = piece(z - i, b)
        return remote(dst if src is None else src, dst, up_send.at[i, b], up_recv.at[i, b], {"dp": me + CORES})

    def down(i, b, src=None):
        dst = piece(z + i, b)
        return remote(dst if src is None else src, dst, down_send.at[i, b], down_recv.at[i, b], {"dp": me - CORES})

    def across(origin, b, src=None):
        dst = piece(origin, b)
        return remote(dst if src is None else src, dst, sib_send.at[origin, b], sib_recv.at[origin, b], {"dp": twin})

    def out_weight(d):
        peer = (spot + d) % n_xy
        return remote(
            ow_hbm.at[pl.ds(core * half, half), pl.ds(pl.multiple_of(peer * wide, wide), wide)],
            wbuf.at[spot, pl.ds(core * half, half)],
            w_send.at[d], w_recv.at[d], {"mp": peer * Z_HI + z_hi},
        )

    def out_weight_across(d):
        origin = (spot + n_xy - d) % n_xy
        where = wbuf.at[origin, pl.ds(core * half, half)]
        return remote(where, where, wsib_send.at[d], wsib_recv.at[d], {"dp": twin})

    for b in range(CHUNKS):
        src = qw_hbm.at[pl.ds(b * bit, bit)]

        @pl.when(z < n_line - 1)
        def _():
            up(0, b, src).start()

        @pl.when(z > 0)
        def _():
            down(0, b, src).start()

    for b in range(CHUNKS):
        across(z, b, qw_hbm.at[pl.ds(b * bit, bit)]).start()

    loads[5].wait()

    def pick(i):
        give[i // CAP, pl.ds(pl.multiple_of(i % CAP * 16, 16), 16), :] = bank[plan_ref[i // CAP, i % CAP]]

    each(0, n_dp * CAP, pick)
    take[me] = give[me]

    loads[0].wait()
    loads[1].wait()
    acc[...] = jnp.zeros_like(acc)

    def multiply(origin):
        columns = pl.ds(pl.multiple_of(origin * shard, shard), shard)
        acc[...] += jnp.dot(hid[:, columns], qbuf[origin], preferred_element_type=F32)

    def multiply_twin(origin):
        for b in range(CHUNKS):
            across(origin, b).wait_recv()
        multiply(origin * CORES + 1 - core)

    multiply(me)
    w_each = -(-(n_xy - 1) // (n_line - 1))

    def line_step(i):
        for b in range(CHUNKS):

            @pl.when(z - i >= 0)
            def _():
                up(i - 1, b).wait_recv()

                @pl.when(z < n_line - 1)
                def _():
                    up(i, b).start()

                across(z - i, b).start()

            @pl.when(z + i < n_line)
            def _():
                down(i - 1, b).wait_recv()

                @pl.when(z > 0)
                def _():
                    down(i, b).start()

                across(z + i, b).start()

        for k in range(w_each):
            d = (i - 1) * w_each + 1 + k

            @pl.when(d < n_xy)
            def _():
                out_weight(d).start()

        @pl.when(z - i >= 0)
        def _():
            multiply((z - i) * CORES + core)

        @pl.when(z + i < n_line)
        def _():
            multiply((z + i) * CORES + core)

        @pl.when(z - i + 1 >= 0)
        def _():
            multiply_twin(z - i + 1)

        @pl.when((z + i - 1 < n_line) & (i > 1))
        def _():
            multiply_twin(z + i - 1)

    each(1, n_line, line_step)

    @pl.when(z == n_line - 1)
    def _():
        multiply_twin(0)

    @pl.when(z == 0)
    def _():
        multiply_twin(n_line - 1)

    def adapters(d):
        peer = dp_peer(d)
        return remote(give.at[peer], take.at[me], give_send.at[d], take_recv.at[d], {"dp": peer})

    each(1, n_dp, lambda d: adapters(d).start())

    def pass_weight(d):
        out_weight(d).wait_recv()
        out_weight_across(d).start()

    each(1, n_xy, pass_weight)

    loads[3].wait()
    loads[4].wait()
    if pad_rows > rows:
        cache[:, prefix_hbm.shape[1] :] = jnp.zeros_like(cache[:, prefix_hbm.shape[1] :])
        qrows[...] = jnp.zeros_like(qrows)
    qrows[0, 0:rows, :] = acc[...].astype(BF16).astype(F32)
    qrows[1, 0:rows, :] = fresh[:, 0, :].astype(F32)
    qrows[2, 0:rows, :] = fresh[:, 1, :].astype(F32)
    block = 8
    tall, keys = block * SAMPLES, block * prefix
    score_scale = 1.0 / math.sqrt(hd)
    own_user = lax.broadcasted_iota(jnp.int32, (tall, keys), 0) // SAMPLES == (
        lax.broadcasted_iota(jnp.int32, (tall, keys), 1) // prefix
    )
    for n in range(users // block):
        at = slice(n * tall, (n + 1) * tall)
        query = qrows[0, at, :]
        key = cache[0, n * block : (n + 1) * block].reshape(keys, hd)
        value = cache[1, n * block : (n + 1) * block].reshape(keys, hd)
        cached = (
            lax.dot_general(query.astype(BF16), key, (((1,), (1,)), ((), ())), preferred_element_type=F32)
            * score_scale
        )
        own_score = jnp.sum(query * qrows[1, at, :], axis=-1, keepdims=True) * score_scale
        cached = jnp.where(own_user, cached, -jnp.inf)
        row_top = jnp.maximum(jnp.max(cached, axis=-1, keepdims=True), own_score)
        cached_exp = jnp.exp(cached - row_top)
        own_exp = jnp.exp(own_score - row_top)
        weight_total = jnp.sum(cached_exp, axis=-1, keepdims=True) + own_exp
        cached_weight = (cached_exp / weight_total).astype(BF16)
        own_weight = (own_exp / weight_total).astype(BF16).astype(F32)
        mixed = jnp.dot(cached_weight, value, preferred_element_type=F32) + own_weight * qrows[2, at, :]
        att[spot, at, :] = mixed.astype(BF16)

    def attended(d):
        return remote(att.at[spot], att.at[spot], att_send.at[d], att_recv.at[d], {"mp": xy_peer(d)})

    each(1, n_xy, lambda d: attended(d).start())
    loads[2].wait()
    each(1, n_xy, lambda d: out_weight_across(d).wait_recv())
    each(1, n_xy, lambda d: attended(d).wait_recv())
    for n in range(0, n_xy, 2):
        left = jnp.concatenate([att[n], att[n + 1]], axis=1)
        right = jnp.concatenate([wbuf[n], wbuf[n + 1]], axis=0)
        term = jnp.dot(left, right, preferred_element_type=F32)
        if n == 0:
            part[...] = term
        else:
            part[...] += term
    for n in range(Z_HI):
        zsend[n] = part[:, n * hd : (n + 1) * hd].astype(BF16)

    def partial_sum(d):
        return remote(zsend.at[(z_hi + d) % Z_HI], zrecv.at[d], z_send.at[d], z_recv.at[d], {"mp": z_peer(d)})

    each(1, Z_HI, lambda d: partial_sum(d).start())

    lane_user = lax.broadcasted_iota(jnp.int32, (1, pad_rows), 1) // SAMPLES

    def place(u, row):
        return jnp.where(lane_user == u, slot_ref[u], row)

    row_slot = lax.fori_loop(0, rows // SAMPLES, place, jnp.full((1, pad_rows), -1, jnp.int32))
    each(1, n_dp, lambda d: adapters(d).wait_recv())
    slots = n_dp * CAP
    maps = take[...].reshape(slots * 16, hd)
    products = lax.dot_general(maps, att[spot], (((1,), (1,)), ((), ())), preferred_element_type=F32)
    products = products.reshape(slots, 16, pad_rows)[:, 0:8, :]
    slot_of = lax.broadcasted_iota(jnp.int32, (slots, 8, pad_rows), 0)
    rank_xy[spot] = jnp.sum(jnp.where(slot_of == row_slot[None], products, 0.0), axis=0)

    def rank_over_xy(d):
        return remote(rank_xy.at[spot], rank_xy.at[spot], rxy_send.at[d], rxy_recv.at[d], {"mp": xy_peer(d)})

    def rank_over_z(d):
        return remote(rank_z.at[z_hi], rank_z.at[z_hi], rz_send.at[d], rz_recv.at[d], {"mp": z_peer(d)})

    each(1, n_xy, lambda d: rank_over_xy(d).start())
    each(1, n_xy, lambda d: rank_over_xy(d).wait_recv())
    rank_z[z_hi] = jnp.sum(rank_xy[...], axis=0)
    each(1, Z_HI, lambda d: rank_over_z(d).start())
    each(1, Z_HI, lambda d: rank_over_z(d).wait_recv())
    rank = jnp.sum(rank_z[...], axis=0).astype(BF16).astype(F32)
    rank = jnp.concatenate([jnp.zeros_like(rank), rank], axis=0)
    slot_of = lax.broadcasted_iota(jnp.int32, (slots, 16, pad_rows), 0)
    spread = jnp.where(slot_of == row_slot[None], rank[None], 0.0).astype(BF16).reshape(slots * 16, pad_rows)
    total = lax.dot_general(spread, maps, (((0,), (0,)), ((), ())), preferred_element_type=F32)
    total += part[:, pl.ds(pl.multiple_of(z_hi * hd, hd), hd)]
    each(1, Z_HI, lambda d: partial_sum(d).wait_recv())
    for d in range(1, Z_HI):
        total += zrecv[d].astype(F32)
    out_ref[...] = total[0:rows].astype(BF16)

    for b in range(CHUNKS):
        for i in range(n_line):

            @pl.when((z < n_line - 1) & (z - i >= 0))
            def _():
                up(i, b).wait_send()

            @pl.when((z > 0) & (z + i < n_line))
            def _():
                down(i, b).wait_send()

        each(0, n_line, lambda o: across(o, b).wait_send())

    def sent(d):
        out_weight(d).wait_send()
        out_weight_across(d).wait_send()
        attended(d).wait_send()
        rank_over_xy(d).wait_send()

    each(1, n_xy, sent)
    each(1, n_dp, lambda d: adapters(d).wait_send())
    each(1, Z_HI, lambda d: partial_sum(d).wait_send())
    each(1, Z_HI, lambda d: rank_over_z(d).wait_send())


def body(
    n_dp, n_mp,
    hidden_rows, query_weight, output_weight, new_kv, prefix_kv, adapter_bank, send_plan, user_slot,
):
    rows = hidden_rows.shape[0]
    shard, hd = query_weight.shape
    n_xy, n_line = n_mp // Z_HI, n_dp // CORES
    prefix = prefix_kv.shape[3]
    users = -(-(rows // SAMPLES) // 8) * 8
    pad_rows = users * SAMPLES
    wide = output_weight.shape[1] // n_xy
    owned = adapter_bank.shape[0]
    bank = adapter_bank.reshape(owned, 16, hd)
    dma = pltpu.SemaphoreType.DMA
    hbm = pl.BlockSpec(memory_space=pl.ANY)
    smem = pl.BlockSpec(memory_space=pltpu.SMEM)
    vmem = pl.BlockSpec(memory_space=pltpu.VMEM)
    return pl.pallas_call(
        functools.partial(kernel, GROUP),
        out_shape=jax.ShapeDtypeStruct((rows, hd), BF16),
        in_specs=[smem, smem, hbm, hbm, hbm, hbm, hbm, hbm],
        out_specs=vmem,
        scratch_shapes=[
            pltpu.VMEM(hidden_rows.shape, BF16),
            pltpu.VMEM((n_dp, shard, hd), BF16),
            pltpu.VMEM((rows, hd), F32),
            pltpu.VMEM((n_xy, hd, wide), BF16),
            pltpu.VMEM((rows, 2, hd), BF16),
            pltpu.VMEM((2, users, prefix, hd), BF16),
            pltpu.VMEM((owned, 16, hd), BF16),
            pltpu.VMEM((n_dp, CAP * 16, hd), BF16),
            pltpu.VMEM((n_dp, CAP * 16, hd), BF16),
            pltpu.VMEM((3, pad_rows, hd), F32),
            pltpu.VMEM((n_xy, pad_rows, hd), BF16),
            pltpu.VMEM((pad_rows, wide), F32),
            pltpu.VMEM((Z_HI, pad_rows, hd), BF16),
            pltpu.VMEM((Z_HI, pad_rows, hd), BF16),
            pltpu.VMEM((n_xy, 8, pad_rows), F32),
            pltpu.VMEM((Z_HI, 8, pad_rows), F32),
            dma((6,)),
            dma((n_line, CHUNKS)),
            dma((n_line, CHUNKS)),
            dma((n_line, CHUNKS)),
            dma((n_line, CHUNKS)),
            dma((n_line, CHUNKS)),
            dma((n_line, CHUNKS)),
            dma((n_xy,)),
            dma((n_xy,)),
            dma((n_xy,)),
            dma((n_xy,)),
            dma((n_dp,)),
            dma((n_dp,)),
            dma((n_xy,)),
            dma((n_xy,)),
            dma((Z_HI,)),
            dma((Z_HI,)),
            dma((n_xy,)),
            dma((n_xy,)),
            dma((Z_HI,)),
            dma((Z_HI,)),
        ],
        compiler_params=pltpu.CompilerParams(
            collective_id=0, has_side_effects=True, vmem_limit_bytes=60 * 1024 * 1024
        ),
    )(send_plan[0], user_slot, hidden_rows, query_weight, output_weight, jnp.transpose(new_kv, (1, 0, 2)), prefix_kv, bank)


def solution(mesh):
    return jax.shard_map(
        functools.partial(body, mesh.shape["dp"], mesh.shape["mp"]),
        mesh=mesh,
        in_specs=(
            P("dp", None),
            P("dp", "mp"),
            P("mp", None),
            P(None, "dp", None),
            P(None, "dp", None, None, None),
            P("dp", None, None, "mp"),
            P("dp", None, None),
            P("dp"),
        ),
        out_specs=P("dp", "mp"),
        check_vma=False,
    )
```

```python
import functools
import math

import jax
import jax.numpy as jnp
from jax import lax
from jax.experimental import pallas as pl
from jax.experimental.pallas import tpu as pltpu
from jax.sharding import PartitionSpec as P

SAMPLES = 4
GROUP = 8
CAP = 5
CORES = 2
Z_HI = 4
CHUNKS = 4
HALVES = 2
F32 = jnp.float32
BF16 = jnp.bfloat16


def each(first, last, step):
    def wrapped(i, carry):
        step(i)
        return carry

    lax.fori_loop(first, last, wrapped, 0)


def kernel(
    group,
    plan_ref, slot_ref, hid_hbm, qw_hbm, ow_hbm, new_hbm, prefix_hbm, bank_hbm,
    out_ref,
    hid, qbuf, acc, wbuf, fresh, cache, bank, give, take, qrows, att, part, zsend, zrecv,
    rank_xy, rank_z,
    local_sem, up_send, up_recv, down_send, down_recv, sib_send, sib_recv,
    w_send, w_recv, wsib_send, wsib_recv, give_send, take_recv, att_send, att_recv,
    z_send, z_recv, rxy_send, rxy_recv, rz_send, rz_recv, ring_sem,
):
    n_dp = qbuf.shape[0]
    n_xy = wbuf.shape[0]
    n_line = n_dp // CORES
    rows = hid.shape[0]
    shard = qbuf.shape[1]
    hd = qbuf.shape[2]
    users = cache.shape[1]
    prefix = cache.shape[2]
    pad_rows = att.shape[1]
    half = hd // CORES
    wide = wbuf.shape[2]
    bit = shard // CHUNKS

    me = lax.axis_index("dp")
    mp = lax.axis_index("mp")
    z, core = me // CORES, me % CORES
    spot, z_hi = mp // Z_HI, mp % Z_HI
    twin = z * CORES + (1 - core)
    kv = mp // group

    def dp_peer(d):
        return (me + d) % n_dp

    def xy_peer(d):
        return ((spot + d) % n_xy) * Z_HI + z_hi

    def z_peer(d):
        return spot * Z_HI + (z_hi + d) % Z_HI

    loads = [
        pltpu.make_async_copy(hid_hbm, hid, local_sem.at[0]),
        pltpu.make_async_copy(qw_hbm, qbuf.at[me], local_sem.at[1]),
        pltpu.make_async_copy(
            ow_hbm.at[:, pl.ds(pl.multiple_of(spot * wide, wide), wide)], wbuf.at[spot], local_sem.at[2]
        ),
        pltpu.make_async_copy(
            new_hbm.at[:, :, pl.ds(pl.multiple_of(kv * hd, hd), hd)], fresh, local_sem.at[3]
        ),
        pltpu.make_async_copy(prefix_hbm.at[:, :, kv], cache.at[:, pl.ds(0, prefix_hbm.shape[1])], local_sem.at[4]),
        pltpu.make_async_copy(bank_hbm, bank, local_sem.at[5]),
    ]
    for load in loads:
        load.start()

    barrier = pltpu.get_barrier_semaphore()

    def greet(peer):
        pl.semaphore_signal(barrier, inc=1, device_id=peer, device_id_type=pl.DeviceIdType.MESH)

    n_ring = n_line * Z_HI

    def ring_peer(d):
        at = (z_hi * n_line + z + d + n_ring) % n_ring
        return {"dp": at % n_line * CORES + core, "mp": spot * Z_HI + at // n_line}

    greet(ring_peer(1))
    greet(ring_peer(-1))
    greet({"dp": twin})
    each(1, n_xy, lambda d: greet({"mp": xy_peer(d)}))
    pl.semaphore_wait(barrier, n_xy + 2)

    stages = ring_sem.shape[0]

    def tell(k):
        for d in (2**k, -(2**k)):
            pl.semaphore_signal(
                ring_sem.at[k], inc=1, device_id=ring_peer(d), device_id_type=pl.DeviceIdType.MESH
            )

    def heard(k):
        pl.semaphore_wait(ring_sem.at[k], 2)
        if k + 1 < stages:
            tell(k + 1)

    tell(0)

    def remote(src, dst, send_sem, recv_sem, peer):
        return pltpu.make_async_remote_copy(
            src_ref=src, dst_ref=dst, send_sem=send_sem, recv_sem=recv_sem,
            device_id=peer, device_id_type=pl.DeviceIdType.MESH,
        )

    def piece(origin, b):
        return qbuf.at[origin * CORES + core, pl.ds(b * bit, bit)]

    def up(i, b, src=None):
        dst = piece(z - i, b)
        return remote(dst if src is None else src, dst, up_send.at[i, b], up_recv.at[i, b], {"dp": me + CORES})

    def down(i, b, src=None):
        dst = piece(z + i, b)
        return remote(dst if src is None else src, dst, down_send.at[i, b], down_recv.at[i, b], {"dp": me - CORES})

    def across(origin, b, src=None):
        dst = piece(origin, b)
        return remote(dst if src is None else src, dst, sib_send.at[origin, b], sib_recv.at[origin, b], {"dp": twin})

    def out_weight(d):
        peer = (spot + d) % n_xy
        return remote(
            ow_hbm.at[pl.ds(core * half, half), pl.ds(pl.multiple_of(peer * wide, wide), wide)],
            wbuf.at[spot, pl.ds(core * half, half)],
            w_send.at[d], w_recv.at[d], {"mp": peer * Z_HI + z_hi},
        )

    def out_weight_across(d):
        origin = (spot + n_xy - d) % n_xy
        where = wbuf.at[origin, pl.ds(core * half, half)]
        return remote(where, where, wsib_send.at[d], wsib_recv.at[d], {"dp": twin})

    for b in range(CHUNKS):
        src = qw_hbm.at[pl.ds(b * bit, bit)]

        @pl.when(z < n_line - 1)
        def _():
            up(0, b, src).start()

        @pl.when(z > 0)
        def _():
            down(0, b, src).start()

    for b in range(CHUNKS):
        across(z, b, qw_hbm.at[pl.ds(b * bit, bit)]).start()

    loads[5].wait()

    def pick(i):
        give[i // CAP, pl.ds(pl.multiple_of(i % CAP * 16, 16), 16), :] = bank[plan_ref[i % CAP, 0, i // CAP]]

    each(0, n_dp * CAP, pick)
    take[me] = give[me]

    loads[0].wait()
    loads[1].wait()
    acc[...] = jnp.zeros_like(acc)

    def multiply(origin):
        for b in range(CHUNKS):
            across(origin, b).wait_recv()
        columns = pl.ds(pl.multiple_of(origin * CORES * shard, CORES * shard), CORES * shard)
        pair = qbuf[pl.ds(origin * CORES, CORES)].reshape(CORES * shard, hd)
        acc[...] += jnp.dot(hid[:, columns], pair, preferred_element_type=F32)

    w_each = -(-(n_xy - 1) // (n_line - 1))

    def line_step(i):
        for b in range(CHUNKS):

            @pl.when(z - i >= 0)
            def _():
                up(i - 1, b).wait_recv()

                @pl.when(z < n_line - 1)
                def _():
                    up(i, b).start()

                across(z - i, b).start()

            @pl.when(z + i < n_line)
            def _():
                down(i - 1, b).wait_recv()

                @pl.when(z > 0)
                def _():
                    down(i, b).start()

                across(z + i, b).start()

            if b == CHUNKS // 2 - 1:

                @pl.when(z - i + 1 >= 0)
                def _():
                    multiply(z - i + 1)

            if b == CHUNKS - 1:

                @pl.when((z + i - 1 < n_line) & (i > 1))
                def _():
                    multiply(z + i - 1)

        for k in range(stages):
            if 2**k < n_line:

                @pl.when(i == 2**k)
                def _():
                    heard(k)

        for k in range(w_each):
            d = (i - 1) * w_each + 1 + k

            @pl.when(d < n_xy)
            def _():
                out_weight(d).start()

    each(1, n_line, line_step)

    @pl.when(z == n_line - 1)
    def _():
        multiply(0)

    @pl.when(z == 0)
    def _():
        multiply(n_line - 1)

    for k in range(stages):
        if 2**k >= n_line:
            heard(k)

    def adapters(d):
        peer = dp_peer(d)
        return remote(give.at[peer], take.at[me], give_send.at[d], take_recv.at[d], {"dp": peer})

    each(1, n_dp, lambda d: adapters(d).start())

    def pass_weight(d):
        out_weight(d).wait_recv()
        out_weight_across(d).start()

    each(1, n_xy, pass_weight)

    loads[3].wait()
    loads[4].wait()
    if pad_rows > rows:
        cache[:, prefix_hbm.shape[1] :] = jnp.zeros_like(cache[:, prefix_hbm.shape[1] :])
        qrows[...] = jnp.zeros_like(qrows)
    qrows[0, 0:rows, :] = acc[...].astype(BF16).astype(F32)
    qrows[1, 0:rows, :] = fresh[:, 0, :].astype(F32)
    qrows[2, 0:rows, :] = fresh[:, 1, :].astype(F32)
    block = 8
    tall, keys = block * SAMPLES, block * prefix
    score_scale = 1.0 / math.sqrt(hd)
    own_user = lax.broadcasted_iota(jnp.int32, (tall, keys), 0) // SAMPLES == (
        lax.broadcasted_iota(jnp.int32, (tall, keys), 1) // prefix
    )
    for n in range(users // block):
        at = slice(n * tall, (n + 1) * tall)
        query = qrows[0, at, :]
        key = cache[0, n * block : (n + 1) * block].reshape(keys, hd)
        value = cache[1, n * block : (n + 1) * block].reshape(keys, hd)
        cached = (
            lax.dot_general(query.astype(BF16), key, (((1,), (1,)), ((), ())), preferred_element_type=F32)
            * score_scale
        )
        own_score = jnp.sum(query * qrows[1, at, :], axis=-1, keepdims=True) * score_scale
        cached = jnp.where(own_user, cached, -jnp.inf)
        row_top = jnp.maximum(jnp.max(cached, axis=-1, keepdims=True), own_score)
        cached_exp = jnp.exp(cached - row_top)
        own_exp = jnp.exp(own_score - row_top)
        weight_total = jnp.sum(cached_exp, axis=-1, keepdims=True) + own_exp
        cached_weight = (cached_exp / weight_total).astype(BF16)
        own_weight = (own_exp / weight_total).astype(BF16).astype(F32)
        mixed = jnp.dot(cached_weight, value, preferred_element_type=F32) + own_weight * qrows[2, at, :]
        att[spot, at, :] = mixed.astype(BF16)

    half_rows = pad_rows // HALVES

    def attended(h, d):
        at = att.at[spot, pl.ds(h * half_rows, half_rows)]
        return remote(at, at, att_send.at[h, d], att_recv.at[h, d], {"mp": xy_peer(d)})

    def partial_sum(h, d):
        target = (z_hi + d) % Z_HI
        return remote(zsend.at[h, target], zrecv.at[h, d], z_send.at[h, d], z_recv.at[h, d], {"mp": z_peer(d)})

    def project(h):
        each(1, n_xy, lambda d: attended(h, d).wait_recv())
        at = slice(h * half_rows, (h + 1) * half_rows)
        for n in range(0, n_xy, 2):
            left = jnp.concatenate([att[n, at], att[n + 1, at]], axis=1)
            right = jnp.concatenate([wbuf[n], wbuf[n + 1]], axis=0)
            term = jnp.dot(left, right, preferred_element_type=F32)
            if n == 0:
                part[at] = term
            else:
                part[at] += term
        for n in range(Z_HI):
            zsend[h, n] = part[at, n * hd : (n + 1) * hd].astype(BF16)

    def send_sums(h):
        for d in (2, 1, 3):
            partial_sum(h, d).start()

    for h in range(HALVES):
        each(1, n_xy, lambda d: attended(h, d).start())
    loads[2].wait()
    lane_user = lax.broadcasted_iota(jnp.int32, (1, pad_rows), 1) // SAMPLES

    def place(u, row):
        return jnp.where(lane_user == u, slot_ref[u], row)

    row_slot = lax.fori_loop(0, rows // SAMPLES, place, jnp.full((1, pad_rows), -1, jnp.int32))
    each(1, n_xy, lambda d: out_weight_across(d).wait_recv())
    for h in range(HALVES - 1):
        project(h)
        send_sums(h)

    each(1, n_dp, lambda d: adapters(d).wait_recv())
    slots = n_dp * CAP
    maps = take[...].reshape(slots * 16, hd)
    products = lax.dot_general(maps, att[spot], (((1,), (1,)), ((), ())), preferred_element_type=F32)
    products = products.reshape(slots, 16, pad_rows)[:, 0:8, :]
    slot_of = lax.broadcasted_iota(jnp.int32, (slots, 8, pad_rows), 0)
    rank_xy[spot] = jnp.sum(jnp.where(slot_of == row_slot[None], products, 0.0), axis=0)

    def rank_over_xy(d):
        return remote(rank_xy.at[spot], rank_xy.at[spot], rxy_send.at[d], rxy_recv.at[d], {"mp": xy_peer(d)})

    def rank_over_z(d):
        return remote(rank_z.at[z_hi], rank_z.at[z_hi], rz_send.at[d], rz_recv.at[d], {"mp": z_peer(d)})

    each(1, n_xy, lambda d: rank_over_xy(d).start())
    project(HALVES - 1)
    each(1, n_xy, lambda d: rank_over_xy(d).wait_recv())
    rank_z[z_hi] = jnp.sum(rank_xy[...], axis=0)
    for d in (2, 1, 3):
        rank_over_z(d).start()
    send_sums(HALVES - 1)
    each(1, Z_HI, lambda d: rank_over_z(d).wait_recv())
    rank = jnp.sum(rank_z[...], axis=0).astype(BF16).astype(F32)
    rank = jnp.concatenate([jnp.zeros_like(rank), rank], axis=0)
    slot_of = lax.broadcasted_iota(jnp.int32, (slots, 16, pad_rows), 0)
    spread = jnp.where(slot_of == row_slot[None], rank[None], 0.0).astype(BF16).reshape(slots * 16, pad_rows)
    total = lax.dot_general(spread, maps, (((0,), (0,)), ((), ())), preferred_element_type=F32)
    total += part[:, pl.ds(pl.multiple_of(z_hi * hd, hd), hd)]
    for h in range(HALVES):
        at = slice(h * half_rows, min((h + 1) * half_rows, rows))
        some = total[at]
        for d in (1, 3, 2):
            partial_sum(h, d).wait_recv()
            some += zrecv[h, d, 0 : at.stop - at.start].astype(F32)
        out_ref[at] = some.astype(BF16)

    for b in range(CHUNKS):
        for i in range(n_line):

            @pl.when((z < n_line - 1) & (z - i >= 0))
            def _():
                up(i, b).wait_send()

            @pl.when((z > 0) & (z + i < n_line))
            def _():
                down(i, b).wait_send()

        each(0, n_line, lambda o: across(o, b).wait_send())

    def sent(d):
        out_weight(d).wait_send()
        out_weight_across(d).wait_send()
        rank_over_xy(d).wait_send()

    each(1, n_xy, sent)
    each(1, n_dp, lambda d: adapters(d).wait_send())
    for h in range(HALVES):
        each(1, n_xy, lambda d: attended(h, d).wait_send())
        each(1, Z_HI, lambda d: partial_sum(h, d).wait_send())
    each(1, Z_HI, lambda d: rank_over_z(d).wait_send())


def body(
    n_dp, n_mp,
    hidden_rows, query_weight, output_weight, new_kv, prefix_kv, adapter_bank, send_plan, user_slot,
):
    rows = hidden_rows.shape[0]
    shard, hd = query_weight.shape
    n_xy, n_line = n_mp // Z_HI, n_dp // CORES
    prefix = prefix_kv.shape[3]
    users = -(-(rows // SAMPLES) // 8) * 8
    pad_rows = users * SAMPLES
    wide = output_weight.shape[1] // n_xy
    owned = adapter_bank.shape[0]
    bank = adapter_bank.reshape(owned, 16, hd)
    dma = pltpu.SemaphoreType.DMA
    hbm = pl.BlockSpec(memory_space=pl.ANY)
    smem = pl.BlockSpec(memory_space=pltpu.SMEM)
    vmem = pl.BlockSpec(memory_space=pltpu.VMEM)
    return pl.pallas_call(
        functools.partial(kernel, GROUP),
        out_shape=jax.ShapeDtypeStruct((rows, hd), BF16),
        in_specs=[smem, smem, hbm, hbm, hbm, hbm, hbm, hbm],
        out_specs=vmem,
        scratch_shapes=[
            pltpu.VMEM(hidden_rows.shape, BF16),
            pltpu.VMEM((n_dp, shard, hd), BF16),
            pltpu.VMEM((rows, hd), F32),
            pltpu.VMEM((n_xy, hd, wide), BF16),
            pltpu.VMEM((rows, 2, hd), BF16),
            pltpu.VMEM((2, users, prefix, hd), BF16),
            pltpu.VMEM((owned, 16, hd), BF16),
            pltpu.VMEM((n_dp, CAP * 16, hd), BF16),
            pltpu.VMEM((n_dp, CAP * 16, hd), BF16),
            pltpu.VMEM((3, pad_rows, hd), F32),
            pltpu.VMEM((n_xy, pad_rows, hd), BF16),
            pltpu.VMEM((pad_rows, wide), F32),
            pltpu.VMEM((HALVES, Z_HI, pad_rows // HALVES, hd), BF16),
            pltpu.VMEM((HALVES, Z_HI, pad_rows // HALVES, hd), BF16),
            pltpu.VMEM((n_xy, 8, pad_rows), F32),
            pltpu.VMEM((Z_HI, 8, pad_rows), F32),
            dma((6,)),
            dma((n_line, CHUNKS)),
            dma((n_line, CHUNKS)),
            dma((n_line, CHUNKS)),
            dma((n_line, CHUNKS)),
            dma((n_line, CHUNKS)),
            dma((n_line, CHUNKS)),
            dma((n_xy,)),
            dma((n_xy,)),
            dma((n_xy,)),
            dma((n_xy,)),
            dma((n_dp,)),
            dma((n_dp,)),
            dma((HALVES, n_xy)),
            dma((HALVES, n_xy)),
            dma((HALVES, Z_HI)),
            dma((HALVES, Z_HI)),
            dma((n_xy,)),
            dma((n_xy,)),
            dma((Z_HI,)),
            dma((Z_HI,)),
            pltpu.SemaphoreType.REGULAR(((2 * n_line).bit_length() - 1,)),
        ],
        compiler_params=pltpu.CompilerParams(
            collective_id=0, has_side_effects=True, vmem_limit_bytes=60 * 1024 * 1024
        ),
    )(jnp.transpose(send_plan, (2, 0, 1)), user_slot, hidden_rows, query_weight, output_weight, jnp.transpose(new_kv, (1, 0, 2)), prefix_kv, bank)


def solution(mesh):
    return jax.shard_map(
        functools.partial(body, mesh.shape["dp"], mesh.shape["mp"]),
        mesh=mesh,
        in_specs=(
            P("dp", None),
            P("dp", "mp"),
            P("mp", None),
            P(None, "dp", None),
            P(None, "dp", None, None, None),
            P("dp", None, None, "mp"),
            P("dp", None, None),
            P("dp"),
        ),
        out_specs=P("dp", "mp"),
        check_vma=False,
    )
```

```python
import functools
import math

import jax
import jax.numpy as jnp
from jax import lax
from jax.experimental import pallas as pl
from jax.experimental.pallas import tpu as pltpu
from jax.sharding import PartitionSpec as P

SAMPLES = 4
GROUP = 8
CAP = 5
CORES = 2
Z_HI = 4
CHUNKS = 4
HALVES = 2
LANES = 128
F32 = jnp.float32
BF16 = jnp.bfloat16


def each(first, last, step):
    def wrapped(i, carry):
        step(i)
        return carry

    lax.fori_loop(first, last, wrapped, 0)


def kernel(
    group,
    plan_ref, slot_ref, hid_hbm, qw_hbm, ow_hbm, new_hbm, prefix_hbm, bank_hbm,
    out_ref,
    hid, qbuf, acc, wbuf, fresh, cache, bank, give, take, qrows, att, part, zsend, zrecv,
    rank_xy, rank_z,
    local_sem, up_send, up_recv, down_send, down_recv, sib_send, sib_recv,
    w_send, w_recv, wsib_send, wsib_recv, give_send, take_recv, att_send, att_recv,
    z_send, z_recv, rxy_send, rxy_recv, rz_send, rz_recv, ring_sem, maps_f32, user_up,
):
    n_dp = qbuf.shape[0]
    n_xy = wbuf.shape[0]
    n_line = n_dp // CORES
    rows = hid.shape[0]
    shard = qbuf.shape[1]
    hd = qbuf.shape[2]
    users = cache.shape[1]
    prefix = cache.shape[2]
    pad_rows = att.shape[1]
    half = hd // CORES
    wide = wbuf.shape[2]
    bit = shard // CHUNKS

    me = lax.axis_index("dp")
    mp = lax.axis_index("mp")
    z, core = me // CORES, me % CORES
    spot, z_hi = mp // Z_HI, mp % Z_HI
    twin = z * CORES + (1 - core)
    kv = mp // group

    def dp_peer(d):
        return (me + d) % n_dp

    def xy_peer(d):
        return ((spot + d) % n_xy) * Z_HI + z_hi

    def z_peer(d):
        return spot * Z_HI + (z_hi + d) % Z_HI

    loads = [
        pltpu.make_async_copy(hid_hbm, hid, local_sem.at[0]),
        pltpu.make_async_copy(qw_hbm, qbuf.at[me], local_sem.at[1]),
        pltpu.make_async_copy(
            ow_hbm.at[:, pl.ds(pl.multiple_of(spot * wide, wide), wide)], wbuf.at[spot], local_sem.at[2]
        ),
        pltpu.make_async_copy(
            new_hbm.at[:, :, pl.ds(pl.multiple_of(kv * hd, hd), hd)], fresh, local_sem.at[3]
        ),
        pltpu.make_async_copy(prefix_hbm.at[:, :, kv], cache.at[:, pl.ds(0, prefix_hbm.shape[1])], local_sem.at[4]),
        pltpu.make_async_copy(bank_hbm, bank, local_sem.at[5]),
    ]
    for load in loads:
        load.start()

    barrier = pltpu.get_barrier_semaphore()

    def greet(peer):
        pl.semaphore_signal(barrier, inc=1, device_id=peer, device_id_type=pl.DeviceIdType.MESH)

    n_ring = n_line * Z_HI

    def ring_peer(d):
        at = (z_hi * n_line + z + d + n_ring) % n_ring
        return {"dp": at % n_line * CORES + core, "mp": spot * Z_HI + at // n_line}

    greet(ring_peer(1))
    greet(ring_peer(-1))
    greet({"dp": twin})
    each(1, n_xy, lambda d: greet({"mp": xy_peer(d)}))
    pl.semaphore_wait(barrier, n_xy + 2)

    stages = ring_sem.shape[0]

    def tell(k):
        for d in (2**k, -(2**k)):
            pl.semaphore_signal(
                ring_sem.at[k], inc=1, device_id=ring_peer(d), device_id_type=pl.DeviceIdType.MESH
            )

    def heard(k):
        pl.semaphore_wait(ring_sem.at[k], 2)
        if k + 1 < stages:
            tell(k + 1)

    tell(0)

    def remote(src, dst, send_sem, recv_sem, peer):
        return pltpu.make_async_remote_copy(
            src_ref=src, dst_ref=dst, send_sem=send_sem, recv_sem=recv_sem,
            device_id=peer, device_id_type=pl.DeviceIdType.MESH,
        )

    def piece(origin, b):
        return qbuf.at[origin * CORES + core, pl.ds(b * bit, bit)]

    def up(i, b, src=None):
        dst = piece(z - i, b)
        return remote(dst if src is None else src, dst, up_send.at[i, b], up_recv.at[i, b], {"dp": me + CORES})

    def down(i, b, src=None):
        dst = piece(z + i, b)
        return remote(dst if src is None else src, dst, down_send.at[i, b], down_recv.at[i, b], {"dp": me - CORES})

    def across(origin, b, src=None):
        dst = piece(origin, b)
        return remote(dst if src is None else src, dst, sib_send.at[origin, b], sib_recv.at[origin, b], {"dp": twin})

    def out_weight(d):
        peer = (spot + d) % n_xy
        return remote(
            ow_hbm.at[pl.ds(core * half, half), pl.ds(pl.multiple_of(peer * wide, wide), wide)],
            wbuf.at[spot, pl.ds(core * half, half)],
            w_send.at[d], w_recv.at[d], {"mp": peer * Z_HI + z_hi},
        )

    def out_weight_across(d):
        origin = (spot + n_xy - d) % n_xy
        where = wbuf.at[origin, pl.ds(core * half, half)]
        return remote(where, where, wsib_send.at[d], wsib_recv.at[d], {"dp": twin})

    for b in range(CHUNKS):
        src = qw_hbm.at[pl.ds(b * bit, bit)]

        @pl.when(z < n_line - 1)
        def _():
            up(0, b, src).start()

        @pl.when(z > 0)
        def _():
            down(0, b, src).start()

    for b in range(CHUNKS):
        across(z, b, qw_hbm.at[pl.ds(b * bit, bit)]).start()

    each(1, n_xy, lambda d: out_weight(d).start())

    loads[5].wait()

    def pick(i):
        give[i // CAP, pl.ds(pl.multiple_of(i % CAP * 16, 16), 16), :] = bank[plan_ref[i % CAP, 0, i // CAP]]

    each(0, n_dp * CAP, pick)
    take[me] = give[me]

    loads[0].wait()
    loads[1].wait()
    acc[...] = jnp.zeros_like(acc)

    def multiply(origin):
        for b in range(CHUNKS):
            across(origin, b).wait_recv()
        columns = pl.ds(pl.multiple_of(origin * CORES * shard, CORES * shard), CORES * shard)
        pair = qbuf[pl.ds(origin * CORES, CORES)].reshape(CORES * shard, hd)
        acc[...] += jnp.dot(hid[:, columns], pair, preferred_element_type=F32)

    def line_step(i):
        for b in range(CHUNKS):

            @pl.when(z - i >= 0)
            def _():
                up(i - 1, b).wait_recv()

                @pl.when(z < n_line - 1)
                def _():
                    up(i, b).start()

                across(z - i, b).start()

            @pl.when(z + i < n_line)
            def _():
                down(i - 1, b).wait_recv()

                @pl.when(z > 0)
                def _():
                    down(i, b).start()

                across(z + i, b).start()

            if b == CHUNKS // 2 - 1:

                @pl.when(z - i + 1 >= 0)
                def _():
                    multiply(z - i + 1)

            if b == CHUNKS - 1:

                @pl.when((z + i - 1 < n_line) & (i > 1))
                def _():
                    multiply(z + i - 1)

        for k in range(stages):
            if 2**k < n_line:

                @pl.when(i == 2**k)
                def _():
                    heard(k)

    each(1, n_line, line_step)

    @pl.when(z == n_line - 1)
    def _():
        multiply(0)

    @pl.when(z == 0)
    def _():
        multiply(n_line - 1)

    for k in range(stages):
        if 2**k >= n_line:
            heard(k)

    def adapters(d):
        peer = dp_peer(d)
        return remote(give.at[peer], take.at[me], give_send.at[d], take_recv.at[d], {"dp": peer})

    each(1, n_dp, lambda d: adapters(d).start())

    def pass_weight(d):
        out_weight(d).wait_recv()
        out_weight_across(d).start()

    each(1, n_xy, pass_weight)

    loads[3].wait()
    loads[4].wait()
    if pad_rows > rows:
        cache[:, prefix_hbm.shape[1] :] = jnp.zeros_like(cache[:, prefix_hbm.shape[1] :])
        qrows[...] = jnp.zeros_like(qrows)
    qrows[0, 0:rows, :] = acc[...].astype(BF16).astype(F32)
    qrows[1, 0:rows, :] = fresh[:, 0, :].astype(F32)
    qrows[2, 0:rows, :] = fresh[:, 1, :].astype(F32)
    block = 8
    tall, keys = block * SAMPLES, block * prefix
    score_scale = 1.0 / math.sqrt(hd)
    own_user = lax.broadcasted_iota(jnp.int32, (tall, keys), 0) // SAMPLES == (
        lax.broadcasted_iota(jnp.int32, (tall, keys), 1) // prefix
    )
    for n in range(users // block):
        at = slice(n * tall, (n + 1) * tall)
        query = qrows[0, at, :]
        key = cache[0, n * block : (n + 1) * block].reshape(keys, hd)
        value = cache[1, n * block : (n + 1) * block].reshape(keys, hd)
        cached = (
            lax.dot_general(query.astype(BF16), key, (((1,), (1,)), ((), ())), preferred_element_type=F32)
            * score_scale
        )
        own_score = jnp.sum(query * qrows[1, at, :], axis=-1, keepdims=True) * score_scale
        cached = jnp.where(own_user, cached, -jnp.inf)
        row_top = jnp.maximum(jnp.max(cached, axis=-1, keepdims=True), own_score)
        cached_exp = jnp.exp(cached - row_top)
        own_exp = jnp.exp(own_score - row_top)
        weight_total = jnp.sum(cached_exp, axis=-1, keepdims=True) + own_exp
        cached_weight = (cached_exp / weight_total).astype(BF16)
        own_weight = (own_exp / weight_total).astype(BF16).astype(F32)
        mixed = jnp.dot(cached_weight, value, preferred_element_type=F32) + own_weight * qrows[2, at, :]
        att[spot, at, :] = mixed.astype(BF16)

    half_rows = pad_rows // HALVES

    def attended(h, d):
        at = att.at[spot, pl.ds(h * half_rows, half_rows)]
        return remote(at, at, att_send.at[h, d], att_recv.at[h, d], {"mp": xy_peer(d)})

    def partial_sum(h, d):
        target = (z_hi + d) % Z_HI
        return remote(zsend.at[h, target], zrecv.at[h, d], z_send.at[h, d], z_recv.at[h, d], {"mp": z_peer(d)})

    def project(h):
        at = slice(h * half_rows, (h + 1) * half_rows)
        for n in range(0, n_xy, 2):
            for d in (n, n + 1):
                if d > 0:
                    attended(h, d).wait_recv()
            one, two = (spot + n_xy - n) % n_xy, (spot + n_xy - n - 1) % n_xy
            left = jnp.concatenate([att[one, at], att[two, at]], axis=1)
            right = jnp.concatenate([wbuf[one], wbuf[two]], axis=0)
            term = jnp.dot(left, right, preferred_element_type=F32)
            if n == 0:
                part[at] = term
            else:
                part[at] += term
        for n in range(Z_HI):
            zsend[h, n] = part[at, n * hd : (n + 1) * hd].astype(BF16)

    def send_sums(h):
        for d in (2, 1, 3):
            partial_sum(h, d).start()

    for h in range(HALVES):
        each(1, n_xy, lambda d: attended(h, d).start())
    loads[2].wait()
    lane_user = lax.broadcasted_iota(jnp.int32, (1, pad_rows), 1) // SAMPLES

    def place(u, row):
        return jnp.where(lane_user == u, slot_ref[u], row)

    row_slot = lax.fori_loop(0, rows // SAMPLES, place, jnp.full((1, pad_rows), -1, jnp.int32))
    each(1, n_xy, lambda d: out_weight_across(d).wait_recv())
    for h in range(HALVES - 1):
        project(h)
        send_sums(h)

    each(1, n_dp, lambda d: adapters(d).wait_recv())
    slots = n_dp * CAP
    maps = take[...].reshape(slots * 16, hd)
    products = lax.dot_general(maps, att[spot], (((1,), (1,)), ((), ())), preferred_element_type=F32)
    products = products.reshape(slots, 16, pad_rows)[:, 0:8, :]
    slot_of = lax.broadcasted_iota(jnp.int32, (slots, 8, pad_rows), 0)
    rank_xy[spot] = jnp.sum(jnp.where(slot_of == row_slot[None], products, 0.0), axis=0)

    def rank_over_xy(d):
        return remote(rank_xy.at[spot], rank_xy.at[spot], rxy_send.at[d], rxy_recv.at[d], {"mp": xy_peer(d)})

    def rank_over_z(d):
        return remote(rank_z.at[z_hi], rank_z.at[z_hi], rz_send.at[d], rz_recv.at[d], {"mp": z_peer(d)})

    each(1, n_xy, lambda d: rank_over_xy(d).start())
    project(HALVES - 1)
    each(1, n_xy, lambda d: rank_over_xy(d).wait_recv())
    rank_z[z_hi] = jnp.sum(rank_xy[...], axis=0)
    for d in (2, 1, 3):
        rank_over_z(d).start()
    send_sums(HALVES - 1)

    maps_f32[0 : slots * 16, :] = maps.astype(F32)
    maps_f32[slots * 16 :, :] = jnp.zeros_like(maps_f32[slots * 16 :, :])
    row_user = lax.broadcasted_iota(jnp.int32, (pad_rows, LANES), 0) // SAMPLES

    def place_rows(u, rows_slot):
        return jnp.where(row_user == u, slot_ref[u], rows_slot)

    rows_slot = lax.fori_loop(0, rows // SAMPLES, place_rows, jnp.full((pad_rows, LANES), -1, jnp.int32))
    lane = lax.broadcasted_iota(jnp.int32, (pad_rows, LANES), 1)
    pick_slot = jnp.where(lane == rows_slot, 1.0, 0.0).astype(BF16)
    for j in range(8):
        up_map = maps_f32[pl.ds(8 + j, LANES, stride=16), :].astype(BF16)
        user_up[j] = jnp.dot(pick_slot, up_map, preferred_element_type=F32)

    for b in range(CHUNKS):
        for i in range(n_line):

            @pl.when((z < n_line - 1) & (z - i >= 0))
            def _():
                up(i, b).wait_send()

            @pl.when((z > 0) & (z + i < n_line))
            def _():
                down(i, b).wait_send()

        each(0, n_line, lambda o: across(o, b).wait_send())

    def sent(d):
        out_weight(d).wait_send()
        out_weight_across(d).wait_send()
        rank_over_xy(d).wait_send()

    each(1, n_xy, sent)
    each(1, n_dp, lambda d: adapters(d).wait_send())
    for h in range(HALVES):
        each(1, n_xy, lambda d: attended(h, d).wait_send())

    each(1, Z_HI, lambda d: rank_over_z(d).wait_recv())
    rank = jnp.sum(rank_z[...], axis=0)
    rank = jnp.concatenate([rank, jnp.zeros_like(rank)], axis=0).astype(BF16)
    which = lax.broadcasted_iota(jnp.int32, (16, 8 * hd), 0)
    over = lax.broadcasted_iota(jnp.int32, (16, 8 * hd), 1) // hd
    ones = jnp.where(which == over, 1.0, 0.0).astype(BF16)
    spread = lax.dot_general(rank, ones, (((0,), (0,)), ((), ())), preferred_element_type=F32)
    total = spread[:, 0:hd] * user_up[0]
    for j in range(1, 8):
        total += spread[:, j * hd : (j + 1) * hd] * user_up[j]
    total += part[:, pl.ds(pl.multiple_of(z_hi * hd, hd), hd)]
    for h in range(HALVES):
        at = slice(h * half_rows, min((h + 1) * half_rows, rows))
        some = total[at]
        for d in (1, 3, 2):
            partial_sum(h, d).wait_recv()
            some += zrecv[h, d, 0 : at.stop - at.start].astype(F32)
        out_ref[at] = some.astype(BF16)

    for h in range(HALVES):
        each(1, Z_HI, lambda d: partial_sum(h, d).wait_send())
    each(1, Z_HI, lambda d: rank_over_z(d).wait_send())

def body(
    n_dp, n_mp,
    hidden_rows, query_weight, output_weight, new_kv, prefix_kv, adapter_bank, send_plan, user_slot,
):
    rows = hidden_rows.shape[0]
    shard, hd = query_weight.shape
    n_xy, n_line = n_mp // Z_HI, n_dp // CORES
    prefix = prefix_kv.shape[3]
    users = -(-(rows // SAMPLES) // 8) * 8
    pad_rows = users * SAMPLES
    wide = output_weight.shape[1] // n_xy
    owned = adapter_bank.shape[0]
    bank = adapter_bank.reshape(owned, 16, hd)
    dma = pltpu.SemaphoreType.DMA
    hbm = pl.BlockSpec(memory_space=pl.ANY)
    smem = pl.BlockSpec(memory_space=pltpu.SMEM)
    vmem = pl.BlockSpec(memory_space=pltpu.VMEM)
    return pl.pallas_call(
        functools.partial(kernel, GROUP),
        out_shape=jax.ShapeDtypeStruct((rows, hd), BF16),
        in_specs=[smem, smem, hbm, hbm, hbm, hbm, hbm, hbm],
        out_specs=vmem,
        scratch_shapes=[
            pltpu.VMEM(hidden_rows.shape, BF16),
            pltpu.VMEM((n_dp, shard, hd), BF16),
            pltpu.VMEM((rows, hd), F32),
            pltpu.VMEM((n_xy, hd, wide), BF16),
            pltpu.VMEM((rows, 2, hd), BF16),
            pltpu.VMEM((2, users, prefix, hd), BF16),
            pltpu.VMEM((owned, 16, hd), BF16),
            pltpu.VMEM((n_dp, CAP * 16, hd), BF16),
            pltpu.VMEM((n_dp, CAP * 16, hd), BF16),
            pltpu.VMEM((3, pad_rows, hd), F32),
            pltpu.VMEM((n_xy, pad_rows, hd), BF16),
            pltpu.VMEM((pad_rows, wide), F32),
            pltpu.VMEM((HALVES, Z_HI, pad_rows // HALVES, hd), BF16),
            pltpu.VMEM((HALVES, Z_HI, pad_rows // HALVES, hd), BF16),
            pltpu.VMEM((n_xy, 8, pad_rows), F32),
            pltpu.VMEM((Z_HI, 8, pad_rows), F32),
            dma((6,)),
            dma((n_line, CHUNKS)),
            dma((n_line, CHUNKS)),
            dma((n_line, CHUNKS)),
            dma((n_line, CHUNKS)),
            dma((n_line, CHUNKS)),
            dma((n_line, CHUNKS)),
            dma((n_xy,)),
            dma((n_xy,)),
            dma((n_xy,)),
            dma((n_xy,)),
            dma((n_dp,)),
            dma((n_dp,)),
            dma((HALVES, n_xy)),
            dma((HALVES, n_xy)),
            dma((HALVES, Z_HI)),
            dma((HALVES, Z_HI)),
            dma((n_xy,)),
            dma((n_xy,)),
            dma((Z_HI,)),
            dma((Z_HI,)),
            pltpu.SemaphoreType.REGULAR(((2 * n_line).bit_length() - 1,)),
            pltpu.VMEM((LANES * 16 + 16, hd), F32),
            pltpu.VMEM((8, pad_rows, hd), F32),
        ],
        compiler_params=pltpu.CompilerParams(
            collective_id=0, has_side_effects=True, vmem_limit_bytes=60 * 1024 * 1024
        ),
    )(jnp.transpose(send_plan, (2, 0, 1)), user_slot, hidden_rows, query_weight, output_weight, jnp.transpose(new_kv, (1, 0, 2)), prefix_kv, bank)


def solution(mesh):
    return jax.shard_map(
        functools.partial(body, mesh.shape["dp"], mesh.shape["mp"]),
        mesh=mesh,
        in_specs=(
            P("dp", None),
            P("dp", "mp"),
            P("mp", None),
            P(None, "dp", None),
            P(None, "dp", None, None, None),
            P("dp", None, None, "mp"),
            P("dp", None, None),
            P("dp"),
        ),
        out_specs=P("dp", "mp"),
        check_vma=False,
    )
```
